32 devices in a mesh: dp: 4 (over z), tensor: 8 (over y, x, core).
Axes of the slice: x: 2, y: 2, z: 4, core: 2. Of those that a mesh axis runs over, the one named last changes fastest.
Arguments:
- q_rows: bfloat16 [256, 1024], P('dp', 'tensor'), parts along dimension 0, may hold values from -160 to 160, as said below
- k_cache: bfloat16 [16, 2048, 512], P('dp', 'tensor'), parts along dimension 0, may hold values from -6 to 6
- v_cache: bfloat16 [16, 2048, 512], P('dp', 'tensor'), parts along dimension 0, may hold values from -24 to 24
- k_tree: bfloat16 [16, 16, 512], P('dp'), parts along dimension 0, may hold values from -18 to 18
- v_tree: bfloat16 [16, 16, 512], P('dp'), parts along dimension 0, may hold values from -24 to 24
- residual: bfloat16 [256, 8192], P('dp', 'tensor'), parts along dimension 0, may hold values from -2 to 2
- wo_rows: bfloat16 [1024, 8192], P('tensor'), may hold values from -1 to 1
- gain: bfloat16 [8192], P('tensor'), may hold values from 0.099609375 to 1.8984375
- parents: int32 [16, 16], P('dp'), parts along dimension 0, may hold values from 0 to 6, as said below
- cache_len: int32 [16], P('dp'), parts along dimension 0, may hold values from 256 to 2048, as said below
- accepted_node: int32 [16], P('dp'), parts along dimension 0, may hold values from 0 to 15, as said below
Outputs:
- layer_out: bfloat16 [256, 8192], P('dp', 'tensor'), parts along dimension 0
- draft_feat: bfloat16 [16, 8, 8192], P('dp', None, 'tensor'), parts along dimension 0
The draws below stay inside these ranges and needn't reach their ends.
There are 4 independent parts, one for each index of `dp`. The reference program is written for one: setup_inputs(seed, part) draws one part's arguments, and reference() takes and returns one part's arrays. A program takes and returns all parts, laid end to end along the dimension named above; an argument that names none is the same for every part. Nothing has to cross between parts.
Inputs may be any that keep to these rules, and one draw needn't show every extreme that they name: `q_rows`: float queries of order one; in the hidden draw some rows are scaled up strongly. `parents`: nodes 1 to 7 form a chain (parent of node i is i - 1); every later node has a parent below 7; entry 0 is 0. `cache_len`: in every group some request has all 2048 positions valid. `accepted_node`: in every group some request accepts node 7, whose path holds 8 nodes.
All inputs are finite; a program needn't handle non-finite values.
Results may differ from the reference program's by a relative error of at most 0.0075.
Values may be sent and summed in bfloat16 or wider, within the bound.
A program may use at most 64 MiB of HBM per device.

```python
import jax
import jax.numpy as jnp
from jax import lax

D = 8192
HD = 128
HEADS_DEV = 1
KVH = 4
REQ = 4
TREE = 16
MAXACC = 8
HEADS = 8
CACHE = 2048
ROWS = 64


def draw_q_rows(key, part):
    base = jax.random.truncated_normal(key, -4.0, 4.0, (ROWS, HEADS * HD), jnp.float32)
    return base.astype(jnp.bfloat16)


def value_offsets(key):
    means = jax.random.uniform(jax.random.fold_in(key, 23), (HD,), jnp.float32, 0.3, 1.0)
    return jnp.tile(means, KVH)


def value_noise(key, shape):
    noise = 4.0 * jax.random.truncated_normal(key, -5.75, 5.75, shape, jnp.float32)
    return noise


def draw_v_cache(key, part):
    noise = value_noise(jax.random.fold_in(key, 21), (REQ, CACHE, KVH * HD))
    return (noise + value_offsets(key)[None, None, :]).astype(jnp.bfloat16)


def draw_v_tree(key, part):
    noise = value_noise(jax.random.fold_in(key, 22), (REQ, TREE, KVH * HD))
    return (noise + value_offsets(key)[None, None, :]).astype(jnp.bfloat16)


def draw_wo_rows(key, part):
    fan = HEADS * HD
    tensor_count = HEADS // HEADS_DEV
    row_block = jnp.arange(fan, dtype=jnp.int32) // (HEADS_DEV * HD)
    col_block = jnp.arange(D, dtype=jnp.int32) // (D // tensor_count)
    pairing = jax.random.permutation(jax.random.fold_in(key, 41), tensor_count).astype(jnp.int32)
    boost = jnp.where(pairing[row_block][:, None] == col_block[None, :], 3.0, 1.0)
    noise = jax.random.truncated_normal(key, -3.0, 3.0, (fan, D), jnp.float32)
    signs = (2 * jax.random.randint(jax.random.fold_in(key, 42), (D,), 0, 2) - 1).astype(jnp.float32)
    return (noise * boost * fan ** (-0.5) + signs[None, :] * (1.5 / fan)).astype(jnp.bfloat16)


def draw_parents(key, part):
    nodes = jnp.arange(TREE, dtype=jnp.int32)
    later = jax.random.randint(key, (REQ, TREE), 0, MAXACC - 1)
    chain = jnp.maximum(nodes - 1, 0)
    return jnp.where(nodes[None, :] < MAXACC, chain[None, :], later).astype(jnp.int32)


def draw_cache_len(key, part):
    lengths = jax.random.randint(key, (REQ,), CACHE // 8, CACHE + 1)
    fullest = jax.random.randint(jax.random.fold_in(key, 5), (), 0, REQ)
    return jnp.where(jnp.arange(REQ, dtype=jnp.int32) == fullest, CACHE, lengths).astype(jnp.int32)


def draw_accepted_node(key, part):
    chosen = jax.random.randint(key, (REQ,), 0, TREE)
    deepest = jax.random.randint(jax.random.fold_in(key, 9), (), 0, REQ)
    return jnp.where(jnp.arange(REQ, dtype=jnp.int32) == deepest, MAXACC - 1, chosen).astype(jnp.int32)


def shard_levels(stream_key, shape, pieces, smallest, high):
    level, own = 1.0, jax.random.fold_in(stream_key, 6)
    for dim, blocks in pieces:
        heights = jnp.exp(jax.random.uniform(jax.random.fold_in(own, dim), (blocks,), jnp.float32, smallest / len(pieces), high / len(pieces)))
        level = level * jnp.repeat(heights, shape[dim] // blocks).reshape([-1 if axis == dim else 1 for axis in range(len(shape))])
    return level


def scatter_about(stream_key, shape, scale, bound, pieces=(), kind=jnp.bfloat16):
    entries = scale * jax.random.normal(stream_key, shape, jnp.float32)
    if pieces:
        entries = entries * shard_levels(stream_key, shape, pieces, -0.22, 0.18)
    return jnp.clip(entries, -bound, bound).astype(kind)


def setup_inputs(seed: int = 0, part: int = 0) -> dict:
    arg_keys = jax.random.split(jax.random.key(seed), 12)
    own_keys = jax.random.split(jax.random.fold_in(arg_keys[11], part), 12)
    return {
        "q_rows": draw_q_rows(jax.random.fold_in(jax.random.fold_in(arg_keys[11], part), 71), part),
        "k_cache": scatter_about(own_keys[1], (REQ, CACHE, KVH * HD), 1.0, 6.0, ((1, 8),)),
        "v_cache": draw_v_cache(jax.random.fold_in(jax.random.fold_in(arg_keys[11], part), 71), part),
        "k_tree": scatter_about(own_keys[3], (REQ, TREE, KVH * HD), 3.0, 18.0),
        "v_tree": draw_v_tree(jax.random.fold_in(jax.random.fold_in(arg_keys[11], part), 71), part),
        "residual": scatter_about(own_keys[5], (ROWS, D), 0.3, 2.0, ((1, 8),)),
        "wo_rows": draw_wo_rows(jax.random.fold_in(arg_keys[11], 71), part),
        "gain": jnp.clip(1.0 + 0.18 * jax.random.normal(arg_keys[7], (D,), jnp.float32), 0.099609375, 1.8984375).astype(jnp.bfloat16),
        "parents": draw_parents(jax.random.fold_in(jax.random.fold_in(arg_keys[11], part), 71), part),
        "cache_len": draw_cache_len(jax.random.fold_in(jax.random.fold_in(arg_keys[11], part), 71), part),
        "accepted_node": draw_accepted_node(jax.random.fold_in(jax.random.fold_in(arg_keys[11], part), 71), part),
    }


floor_score = -1e+30
epsilon = 1e-05

def ancestors(parents):
    nodes = jnp.arange(TREE, dtype=jnp.int32)
    link = (parents[:, :, None] == nodes[None, None, :]) & (nodes[None, :, None] > 0)
    reach = jnp.minimum(jnp.eye(TREE, dtype=jnp.float32)[None] + link.astype(jnp.float32), 1.0)
    for sweep in range((TREE - 1).bit_length()):
        reach = jnp.minimum(jnp.einsum('rab,rbc->rac', reach, reach, precision=lax.Precision.HIGHEST), 1.0)
    return reach

def path_select(reach, accepted_node):
    depth = lax.optimization_barrier(jnp.sum(reach, axis=2)) - 1.0
    onehot = (jnp.arange(TREE, dtype=jnp.int32)[None, :] == accepted_node[:, None]).astype(jnp.float32)
    onpath = jnp.einsum('rt,rtu->ru', onehot, reach, precision=lax.Precision.HIGHEST)
    levels = jnp.arange(MAXACC).astype(jnp.float32)
    return onpath[:, None, :] * (depth[:, None, :] == levels[None, :, None]).astype(jnp.float32)

def reference(q_rows, k_cache, v_cache, k_tree, v_tree, residual, wo_rows, gain, parents, cache_len, accepted_node):
    group_size = HEADS // KVH
    score_scale = HD ** (-0.5)
    highest = lax.Precision.HIGHEST
    q_view = q_rows.astype(jnp.float32).reshape(REQ, TREE, KVH, group_size, HD)
    cache_keys = k_cache.astype(jnp.float32).reshape(REQ, CACHE, KVH, HD)
    cache_values = v_cache.astype(jnp.float32).reshape(REQ, CACHE, KVH, HD)
    tree_keys = k_tree.astype(jnp.float32).reshape(REQ, TREE, KVH, HD)
    tree_values = v_tree.astype(jnp.float32).reshape(REQ, TREE, KVH, HD)
    reach = ancestors(parents)
    cache_scores = jnp.einsum('rtkgd,rckd->kgrtc', q_view, cache_keys, precision=highest) * score_scale
    valid = (jnp.arange(CACHE, dtype=jnp.int32)[None, :] < cache_len[:, None])[None, None, :, None, :]
    cache_scores = jnp.where(valid, cache_scores, floor_score)
    tree_scores = jnp.einsum('rtkgd,rukd->kgrtu', q_view, tree_keys, precision=highest) * score_scale
    tree_valid = (reach > 0.5)[None, None]
    tree_scores = jnp.where(tree_valid, tree_scores, floor_score)
    top = jnp.maximum(lax.optimization_barrier(jnp.max(cache_scores, axis=4)), lax.optimization_barrier(jnp.max(tree_scores, axis=4)))
    cache_weights = jnp.where(valid, jnp.exp(cache_scores - top[..., None]), 0.0)
    tree_weights = jnp.where(tree_valid, jnp.exp(tree_scores - top[..., None]), 0.0)
    denominator = lax.optimization_barrier(jnp.sum(cache_weights, axis=4)) + lax.optimization_barrier(jnp.sum(tree_weights, axis=4))
    total = jnp.einsum('kgrtc,rckd->kgrtd', cache_weights.astype(jnp.bfloat16).astype(jnp.float32), cache_values, precision=highest)
    total = total + jnp.einsum('kgrtu,rukd->kgrtd', tree_weights.astype(jnp.bfloat16).astype(jnp.float32), tree_values, precision=highest)
    attention = (total / denominator[..., None]).astype(jnp.bfloat16)
    attention = jnp.transpose(attention, (2, 3, 0, 1, 4)).reshape(ROWS, HEADS * HD)
    hidden = residual.astype(jnp.float32) + jnp.dot(attention, wo_rows, preferred_element_type=jnp.float32)
    layer_out = hidden.astype(jnp.bfloat16)
    mean_square = lax.optimization_barrier(jnp.mean(hidden * hidden, axis=1))
    features = (hidden * lax.rsqrt(mean_square + epsilon)[:, None] * gain.astype(jnp.float32)[None, :]).astype(jnp.bfloat16)
    select = path_select(reach, accepted_node)
    draft_feat = jnp.einsum('rat,rtc->rac', select, features.astype(jnp.float32).reshape(REQ, TREE, D), precision=highest)
    return (layer_out, draft_feat.astype(jnp.bfloat16))
```

```python
import functools

import jax
import jax.numpy as jnp
from jax import lax
from jax.experimental import pallas as pl
from jax.experimental.pallas import tpu as pltpu
from jax.sharding import PartitionSpec as P

HD = 128
KVH = 4
TREE = 16
MAXACC = 8

FLOOR = -1e30
EPS = 1e-05
F32 = jnp.float32
BF16 = jnp.bfloat16
NT = (((1,), (1,)), ((), ()))


def matmul(a, b):
    return jnp.dot(a, b, preferred_element_type=F32)


def iota(shape, dim):
    return lax.broadcasted_iota(jnp.int32, shape, dim)


def tree_reach(parents, reqs):
    rows = reqs * TREE
    node = iota((TREE, TREE), 0)
    child = iota((TREE, TREE), 1)
    blocks = []
    for r in range(reqs):
        link = (parents[r : r + 1, :] == node) & (child > 0)
        blocks.append(jnp.where(link | (node == child), 1.0, 0.0))
    stacked = jnp.concatenate(blocks, axis=0).astype(BF16)
    spread = jnp.where(iota((TREE, rows), 1) % TREE == iota((TREE, rows), 0), 1.0, 0.0)
    same = iota((rows, rows), 0) // TREE == iota((rows, rows), 1) // TREE
    reach = jnp.where(same, jnp.minimum(matmul(stacked, spread.astype(BF16)), 1.0), 0.0)
    for _ in range((TREE - 1).bit_length()):
        half = reach.astype(BF16)
        reach = jnp.minimum(matmul(half, half), 1.0)
    return reach


def kernel(
    count,
    q_ref,
    k_ref,
    v_ref,
    kt_ref,
    vt_ref,
    res_ref,
    wo_ref,
    gain_ref,
    parents_ref,
    len_ref,
    acc_node_ref,
    out_ref,
    draft_ref,
    q_all,
    k_buf,
    v_buf,
    kt_buf,
    vt_buf,
    res_buf,
    wo_buf,
    acc_send,
    acc_recv,
    stat_send,
    stat_recv,
    att_buf,
    hid_send,
    hid_recv,
    sq_send,
    sq_recv,
    load_sem,
    wo_sem,
    q_ssem,
    q_rsem,
    acc_ssem,
    acc_rsem,
    stat_ssem,
    stat_rsem,
    wx_ssem,
    wx_rsem,
    att_ssem,
    att_rsem,
    hid_ssem,
    hid_rsem,
    sq_ssem,
    sq_rsem,
):
    me = lax.axis_index("tensor")
    parity = me % 2
    pair = me // 2
    partner = me + 1 - 2 * parity
    pairs = count // 2
    reqs, span, _ = k_ref.shape
    rows = reqs * TREE
    group = count // KVH
    grows = group * TREE
    cols = res_ref.shape[1]
    kv_col = pl.multiple_of((me // group) * HD, HD)

    def remote(src, dst, ssem, rsem, peer):
        return pltpu.make_async_remote_copy(
            src_ref=src,
            dst_ref=dst,
            send_sem=ssem,
            recv_sem=rsem,
            device_id={"tensor": peer},
            device_id_type=pl.DeviceIdType.MESH,
        )

    my_rows = pl.ds(pl.multiple_of(me * TREE, TREE), TREE)
    q_own = pltpu.make_async_copy(q_ref, q_all.at[:, my_rows, :], load_sem.at[0])
    q_own.start()
    k_copies = [
        pltpu.make_async_copy(k_ref.at[r], k_buf.at[r], load_sem.at[1 + r]) for r in range(reqs)
    ]
    v_copies = [
        pltpu.make_async_copy(v_ref.at[r], v_buf.at[r], load_sem.at[1 + reqs + r])
        for r in range(reqs)
    ]
    base = 1 + 2 * reqs
    kt_copy = pltpu.make_async_copy(kt_ref.at[:, :, pl.ds(kv_col, HD)], kt_buf, load_sem.at[base])
    vt_copy = pltpu.make_async_copy(
        vt_ref.at[:, :, pl.ds(kv_col, HD)], vt_buf, load_sem.at[base + 1]
    )
    res_copy = pltpu.make_async_copy(res_ref, res_buf, load_sem.at[base + 2])
    for copy in k_copies + v_copies + [kt_copy, vt_copy, res_copy]:
        copy.start()

    barrier = pltpu.get_barrier_semaphore()
    peers = [lax.rem(me + k, count) for k in range(1, count)]
    for peer in peers:
        pl.semaphore_signal(
            barrier, inc=1, device_id={"tensor": peer}, device_id_type=pl.DeviceIdType.MESH
        )
    q_own.wait()
    pl.semaphore_wait(barrier, count - 1)

    mine = q_all.at[:, my_rows, :]
    q_sends = [
        remote(mine, mine, q_ssem.at[k], q_rsem.at[k], peers[k]) for k in range(count - 1)
    ]
    for copy in q_sends:
        copy.start()

    def wo_block(b, who):
        first = pl.multiple_of((2 * b + who) * cols, 128)
        return wo_ref.at[:, pl.ds(first, cols)]

    wx = [
        remote(
            wo_block(b, 1 - parity), wo_buf.at[b, parity], wx_ssem.at[b], wx_rsem.at[b], partner
        )
        for b in range(pairs)
    ]
    wo_copies = [
        pltpu.make_async_copy(wo_block(b, parity), wo_buf.at[b, parity], wo_sem.at[b])
        for b in range(pairs)
    ]
    for copy in wx + wo_copies:
        copy.start()

    kt_copy.wait()
    vt_copy.wait()
    reach_t = tree_reach(parents_ref[...], reqs)
    eye = jnp.where(iota((rows, rows), 0) == iota((rows, rows), 1), 1.0, 0.0).astype(BF16)
    reach = lax.dot_general(eye, reach_t.astype(BF16), NT, preferred_element_type=F32)
    scale = HD ** (-0.5)
    q_mine = q_all[:, my_rows, :].reshape(rows, HD)
    tree_scores = (
        lax.dot_general(q_mine, kt_buf[...].reshape(rows, HD), NT, preferred_element_type=F32)
        * scale
    )
    tree_valid = reach > 0.5
    tree_max = jnp.max(jnp.where(tree_valid, tree_scores, FLOOR), axis=1, keepdims=True)
    tree_w = jnp.where(tree_valid, jnp.exp(tree_scores - tree_max), 0.0)
    tree_sum = jnp.sum(tree_w, axis=1, keepdims=True)
    tree_acc = matmul(tree_w.astype(BF16), vt_buf[...].reshape(rows, HD))

    depth = jnp.sum(reach_t, axis=0, keepdims=True) - 1.0
    slots = reqs * MAXACC
    slot = iota((slots, rows), 0)
    node = iota((slots, rows), 1)
    hit = jnp.zeros((slots, rows), F32)
    for r in range(reqs):
        target = acc_node_ref[r] + r * TREE
        hit = jnp.where((slot // MAXACC == r) & (node == target), 1.0, hit)
    on_path = matmul(hit.astype(BF16), reach.astype(BF16))
    level = (slot % MAXACC).astype(F32)
    select = jnp.where(depth == level, on_path, 0.0).astype(BF16)

    for copy in q_sends:
        copy.wait_recv()

    lane = iota((count * TREE, HD), 1)
    stats = jnp.zeros((count * TREE, HD), F32)
    position = iota((count * TREE, span), 1) + me * span
    for r in range(reqs):
        k_copies[r].wait()
        scores = jnp.concatenate(
            [
                lax.dot_general(
                    q_all[r, g * grows : (g + 1) * grows, :],
                    k_buf[r, :, g * HD : (g + 1) * HD],
                    NT,
                    preferred_element_type=F32,
                )
                for g in range(KVH)
            ],
            axis=0,
        )
        scores = jnp.where(position < len_ref[r], scores * scale, FLOOR)
        top = jnp.max(scores, axis=1, keepdims=True)
        weights = jnp.where(position < len_ref[r], jnp.exp(scores - top), 0.0)
        total = jnp.sum(weights, axis=1, keepdims=True)
        stats = jnp.where(lane == r, top, stats)
        stats = jnp.where(lane == reqs + r, total, stats)
        weights = weights.astype(BF16)
        v_copies[r].wait()
        for g in range(KVH):
            part = matmul(
                weights[g * grows : (g + 1) * grows, :], v_buf[r, :, g * HD : (g + 1) * HD]
            )
            acc_send[g * group : (g + 1) * group, r] = part.astype(BF16).reshape(group, TREE, HD)
    stat_send[...] = stats.reshape(count, TREE, HD)

    acc_sends, stat_sends = [], []
    for k in range(count - 1):
        peer = peers[k]
        stat_sends.append(
            remote(
                stat_send.at[peer], stat_recv.at[k], stat_ssem.at[k], stat_rsem.at[k], peer
            )
        )
        acc_sends.append(
            remote(acc_send.at[peer], acc_recv.at[k], acc_ssem.at[k], acc_rsem.at[k], peer)
        )
        stat_sends[k].start()
        acc_sends[k].start()

    for copy in stat_sends:
        copy.wait_recv()
    all_stats = [stat_send[me]] + [stat_recv[k] for k in range(count - 1)]
    tops = [jnp.concatenate([s[:, r : r + 1] for r in range(reqs)], axis=0) for s in all_stats]
    sums = [
        jnp.concatenate([s[:, reqs + r : reqs + r + 1] for r in range(reqs)], axis=0)
        for s in all_stats
    ]
    peak = tree_max
    for top in tops:
        peak = jnp.maximum(peak, top)
    factor = jnp.exp(tree_max - peak)
    denominator = tree_sum * factor
    numerator = tree_acc * factor
    for k in range(count):
        factor = jnp.exp(tops[k] - peak)
        denominator = denominator + sums[k] * factor
        if k == 0:
            part = acc_send[me]
        else:
            acc_sends[k - 1].wait_recv()
            part = acc_recv[k - 1]
        numerator = numerator + part.reshape(rows, HD).astype(F32) * factor
    att_buf[parity] = (numerator / denominator).astype(BF16)

    att_copy = remote(
        att_buf.at[parity], att_buf.at[parity], att_ssem.at[0], att_rsem.at[0], partner
    )
    att_copy.start()
    for copy in wx:
        copy.wait_recv()
    for copy in wo_copies:
        copy.wait()
    att_copy.wait_recv()
    attention = jnp.concatenate([att_buf[0], att_buf[1]], axis=1)

    hid_sends = []
    for k in range(1, pairs):
        b = lax.rem(pair + pairs - k, pairs)
        hid_send[k - 1] = matmul(attention, wo_buf[b].reshape(2 * HD, cols)).astype(BF16)
        copy = remote(
            hid_send.at[k - 1],
            hid_recv.at[k - 1],
            hid_ssem.at[k - 1],
            hid_rsem.at[k - 1],
            2 * b + parity,
        )
        copy.start()
        hid_sends.append(copy)
    hidden = matmul(attention, wo_buf[pair].reshape(2 * HD, cols))
    res_copy.wait()
    hidden = hidden + res_buf[...].astype(F32)
    for k in range(pairs - 1):
        hid_sends[k].wait_recv()
        hidden = hidden + hid_recv[k].astype(F32)

    square = jnp.sum(hidden * hidden, axis=1, keepdims=True)
    diagonal = iota((rows, HD), 0) == iota((rows, HD), 1)
    sq_send[...] = jnp.broadcast_to(
        jnp.sum(jnp.where(diagonal, square, 0.0), axis=0, keepdims=True), (8, HD)
    )
    sq_sends = [
        remote(sq_send, sq_recv.at[k], sq_ssem.at[k], sq_rsem.at[k], peers[k])
        for k in range(count - 1)
    ]
    for copy in sq_sends:
        copy.start()
    out_ref[...] = hidden.astype(BF16)
    scaled = hidden * gain_ref[...].astype(F32)
    total = sq_send[...]
    for k in range(count - 1):
        sq_sends[k].wait_recv()
        total = total + sq_recv[k]
    mean = jnp.sum(jnp.where(diagonal, total[0:1, :], 0.0), axis=1, keepdims=True) / (cols * count)
    features = (scaled * lax.rsqrt(mean + EPS)).astype(BF16)
    draft_ref[...] = matmul(select, features).astype(BF16).reshape(reqs, MAXACC, cols)

    for copies in (q_sends, wx, stat_sends, acc_sends, [att_copy], hid_sends, sq_sends):
        for copy in copies:
            copy.wait_send()


def on_device(
    count,
    q_rows,
    k_cache,
    v_cache,
    k_tree,
    v_tree,
    residual,
    wo_rows,
    gain,
    parents,
    cache_len,
    accepted_node,
):
    reqs, span, width = k_cache.shape
    rows, cols = residual.shape
    pairs = count // 2
    hbm = pl.BlockSpec(memory_space=pl.ANY)
    vmem = pl.BlockSpec(memory_space=pltpu.VMEM)
    smem = pl.BlockSpec(memory_space=pltpu.SMEM)
    dma = pltpu.SemaphoreType.DMA
    others = count - 1
    return pl.pallas_call(
        functools.partial(kernel, count),
        out_shape=(
            jax.ShapeDtypeStruct((rows, cols), BF16),
            jax.ShapeDtypeStruct((reqs, MAXACC, cols), BF16),
        ),
        in_specs=[hbm] * 7 + [vmem, vmem, smem, smem],
        out_specs=(vmem, vmem),
        scratch_shapes=[
            pltpu.VMEM((reqs, count * TREE, HD), BF16),
            pltpu.VMEM((reqs, span, width), BF16),
            pltpu.VMEM((reqs, span, width), BF16),
            pltpu.VMEM((reqs, TREE, HD), BF16),
            pltpu.VMEM((reqs, TREE, HD), BF16),
            pltpu.VMEM((rows, cols), BF16),
            pltpu.VMEM((pairs, 2, HD, cols), BF16),
            pltpu.VMEM((count, reqs, TREE, HD), BF16),
            pltpu.VMEM((others, reqs, TREE, HD), BF16),
            pltpu.VMEM((count, TREE, HD), F32),
            pltpu.VMEM((others, TREE, HD), F32),
            pltpu.VMEM((2, rows, HD), BF16),
            pltpu.VMEM((pairs - 1, rows, cols), BF16),
            pltpu.VMEM((pairs - 1, rows, cols), BF16),
            pltpu.VMEM((8, HD), F32),
            pltpu.VMEM((others, 8, HD), F32),
            dma((4 + 2 * reqs,)),
            dma((pairs,)),
            dma((others,)),
            dma((others,)),
            dma((others,)),
            dma((others,)),
            dma((others,)),
            dma((others,)),
            dma((pairs,)),
            dma((pairs,)),
            dma((1,)),
            dma((1,)),
            dma((pairs - 1,)),
            dma((pairs - 1,)),
            dma((others,)),
            dma((others,)),
        ],
        compiler_params=pltpu.CompilerParams(
            collective_id=0, has_side_effects=True, vmem_limit_bytes=56 * 2**20
        ),
        name="verify",
    )(
        q_rows.reshape(reqs, TREE, HD),
        k_cache,
        v_cache,
        k_tree,
        v_tree,
        residual,
        wo_rows,
        gain.reshape(1, cols),
        parents,
        cache_len,
        accepted_node,
    )


def solution(mesh):
    return jax.shard_map(
        functools.partial(on_device, mesh.shape["tensor"]),
        mesh=mesh,
        in_specs=(
            P("dp", "tensor"),
            P("dp", "tensor", None),
            P("dp", "tensor", None),
            P("dp", None, None),
            P("dp", None, None),
            P("dp", "tensor"),
            P("tensor", None),
            P("tensor"),
            P("dp", None),
            P("dp"),
            P("dp"),
        ),
        out_specs=(P("dp", "tensor"), P("dp", None, "tensor")),
        check_vma=False,
    )
```

```python
import functools

import jax
import jax.numpy as jnp
from jax import lax
from jax.experimental import pallas as pl
from jax.experimental.pallas import tpu as pltpu
from jax.sharding import PartitionSpec as P

HD = 128
KVH = 4
TREE = 16
MAXACC = 8

FLOOR = -1e30
EPS = 1e-05
F32 = jnp.float32
BF16 = jnp.bfloat16
NT = (((1,), (1,)), ((), ()))


def parts(x):
    high = x.astype(BF16)
    rest = x - high.astype(F32)
    mid = rest.astype(BF16)
    return high, mid, (rest - mid.astype(F32)).astype(BF16)


def full_columns(cols):
    return max(128, cols // 4 // 128 * 128)


def matmul(a, b):
    return jnp.dot(a, b, preferred_element_type=F32)


def iota(shape, dim):
    return lax.broadcasted_iota(jnp.int32, shape, dim)


def tree_reach(parents, reqs):
    rows = reqs * TREE
    node = iota((TREE, TREE), 0)
    child = iota((TREE, TREE), 1)
    blocks = []
    for r in range(reqs):
        link = (parents[r : r + 1, :] == node) & (child > 0)
        blocks.append(jnp.where(link | (node == child), 1.0, 0.0))
    stacked = jnp.concatenate(blocks, axis=0).astype(BF16)
    spread = jnp.where(iota((TREE, rows), 1) % TREE == iota((TREE, rows), 0), 1.0, 0.0)
    same = iota((rows, rows), 0) // TREE == iota((rows, rows), 1) // TREE
    reach = jnp.where(same, jnp.minimum(matmul(stacked, spread.astype(BF16)), 1.0), 0.0)
    for _ in range((TREE - 1).bit_length()):
        half = reach.astype(BF16)
        reach = jnp.minimum(matmul(half, half), 1.0)
    return reach


def kernel(
    count,
    q_ref,
    k_ref,
    v_ref,
    kt_ref,
    vt_ref,
    res_ref,
    wo_ref,
    gain_ref,
    parents_ref,
    len_ref,
    node_ref,
    out_hbm,
    draft_hbm,
    out_ref,
    draft_ref,
    parents_buf,
    len_buf,
    node_buf,
    q_all,
    k_buf,
    v_buf,
    kt_buf,
    vt_buf,
    res_buf,
    wo_buf,
    wf_buf,
    acc_send,
    acc_recv,
    att_buf,
    hid_send,
    hid_recv,
    sq_send,
    sq_recv,
    load_sem,
    wo_sem,
    q_ssem,
    q_rsem,
    acc_ssem,
    acc_rsem,
    wx_ssem,
    wx_rsem,
    wf_ssem,
    wf_rsem,
    att_ssem,
    att_rsem,
    hid_ssem,
    hid_rsem,
    sq_ssem,
    sq_rsem,
    out_sem,
):
    me = lax.axis_index("tensor")
    parity = me % 2
    pair = me // 2
    partner = me + 1 - 2 * parity
    pairs = count // 2
    reqs, span, _ = k_ref.shape
    rows = reqs * TREE
    group = count // KVH
    grows = group * TREE
    cols = res_ref.shape[1]
    full = wf_buf.shape[2]
    some = cols - full
    kv_col = pl.multiple_of((me // group) * HD, HD)

    def remote(src, dst, ssem, rsem, peer):
        return pltpu.make_async_remote_copy(
            src_ref=src,
            dst_ref=dst,
            send_sem=ssem,
            recv_sem=rsem,
            device_id={"tensor": peer},
            device_id_type=pl.DeviceIdType.MESH,
        )

    barrier = pltpu.get_barrier_semaphore()
    peers = [lax.rem(me + k, count) for k in range(1, count)]
    for peer in peers:
        pl.semaphore_signal(
            barrier, inc=1, device_id={"tensor": peer}, device_id_type=pl.DeviceIdType.MESH
        )

    my_rows = pl.ds(pl.multiple_of(me * TREE, TREE), TREE)
    q_own = pltpu.make_async_copy(q_ref, q_all.at[:, my_rows, :], load_sem.at[0])
    q_own.start()
    k_copies = [
        pltpu.make_async_copy(k_ref.at[r], k_buf.at[r], load_sem.at[1 + r]) for r in range(reqs)
    ]
    v_copies = [
        pltpu.make_async_copy(v_ref.at[r], v_buf.at[r], load_sem.at[1 + reqs + r])
        for r in range(reqs)
    ]
    base = 1 + 2 * reqs
    kt_copy = pltpu.make_async_copy(kt_ref.at[:, :, pl.ds(kv_col, HD)], kt_buf, load_sem.at[base])
    vt_copy = pltpu.make_async_copy(
        vt_ref.at[:, :, pl.ds(kv_col, HD)], vt_buf, load_sem.at[base + 1]
    )
    res_copy = pltpu.make_async_copy(res_ref, res_buf, load_sem.at[base + 2])
    small = [
        pltpu.make_async_copy(src, dst, load_sem.at[base + 3 + i])
        for i, (src, dst) in enumerate(
            [
                (parents_ref, parents_buf),
                (node_ref, node_buf),
                (len_ref, len_buf),
            ]
        )
    ]
    for copy in [kt_copy, vt_copy] + small + k_copies + v_copies + [res_copy]:
        copy.start()
    q_own.wait()
    pl.semaphore_wait(barrier, count - 1)

    mine = q_all.at[:, my_rows, :]
    q_sends = [
        remote(mine, mine, q_ssem.at[k], q_rsem.at[k], peers[k]) for k in range(count - 1)
    ]
    for copy in q_sends:
        copy.start()

    def wo_block(b, who):
        first = pl.multiple_of((2 * b + who) * cols, 128)
        return wo_ref.at[:, pl.ds(first, some)]

    def wo_full(owner):
        first = pl.multiple_of(owner * cols + some, 128)
        return wo_ref.at[:, pl.ds(first, full)]

    wx = [
        remote(
            wo_block(b, 1 - parity), wo_buf.at[b, parity], wx_ssem.at[b], wx_rsem.at[b], partner
        )
        for b in range(pairs)
    ]
    wo_copies = [
        pltpu.make_async_copy(wo_block(b, parity), wo_buf.at[b, parity], wo_sem.at[b])
        for b in range(pairs)
    ]
    wf = [
        remote(wo_full(peers[k]), wf_buf.at[me], wf_ssem.at[k], wf_rsem.at[k], peers[k])
        for k in range(count - 1)
    ]
    wo_copies.append(pltpu.make_async_copy(wo_full(me), wf_buf.at[me], wo_sem.at[pairs]))
    for copy in wf + wx + wo_copies:
        copy.start()

    for copy in [kt_copy, vt_copy] + small:
        copy.wait()
    reach_t = tree_reach(parents_buf[...], reqs)
    eye = jnp.where(iota((rows, rows), 0) == iota((rows, rows), 1), 1.0, 0.0).astype(BF16)
    reach = lax.dot_general(eye, reach_t.astype(BF16), NT, preferred_element_type=F32)
    scale = HD ** (-0.5)
    q_mine = q_all[:, my_rows, :].reshape(rows, HD)
    tree_scores = (
        lax.dot_general(q_mine, kt_buf[...].reshape(rows, HD), NT, preferred_element_type=F32)
        * scale
    )
    tree_valid = reach > 0.5
    tree_max = jnp.max(jnp.where(tree_valid, tree_scores, FLOOR), axis=1, keepdims=True)
    tree_w = jnp.where(tree_valid, jnp.exp(tree_scores - tree_max), 0.0)
    tree_sum = jnp.sum(tree_w, axis=1, keepdims=True)
    tree_acc = matmul(tree_w.astype(BF16), vt_buf[...].reshape(rows, HD))

    depth = jnp.sum(reach_t, axis=0, keepdims=True) - 1.0
    slots = reqs * MAXACC
    slot = iota((slots, rows), 0)
    node = iota((slots, rows), 1)
    hit = jnp.zeros((slots, rows), F32)
    for r in range(reqs):
        target = node_buf[r] + r * TREE
        hit = jnp.where((slot // MAXACC == r) & (node == target), 1.0, hit)
    on_path = matmul(hit.astype(BF16), reach.astype(BF16))
    level = (slot % MAXACC).astype(F32)
    select = jnp.where(depth == level, on_path, 0.0).astype(BF16)

    for copy in q_sends:
        copy.wait_recv()

    lane = iota((count * TREE, HD), 1)
    tops = jnp.full((count * TREE, HD), FLOOR, F32)
    sums = jnp.zeros((count * TREE, HD), F32)
    position = iota((count * TREE, span), 1) + me * span
    for r in range(reqs):
        k_copies[r].wait()
        scores = jnp.concatenate(
            [
                lax.dot_general(
                    q_all[r, g * grows : (g + 1) * grows, :],
                    k_buf[r, :, g * HD : (g + 1) * HD],
                    NT,
                    preferred_element_type=F32,
                )
                for g in range(KVH)
            ],
            axis=0,
        )
        scores = jnp.where(position < len_buf[r], scores * scale, FLOOR)
        top = jnp.max(scores, axis=1, keepdims=True)
        weights = jnp.where(position < len_buf[r], jnp.exp(scores - top), 0.0)
        total = jnp.sum(weights, axis=1, keepdims=True)
        tops = jnp.where(lane == r, top, tops)
        sums = jnp.where(lane == r, total, sums)
        weights = weights.astype(BF16)
        v_copies[r].wait()
        for g in range(KVH):
            part = matmul(
                weights[g * grows : (g + 1) * grows, :], v_buf[r, :, g * HD : (g + 1) * HD]
            )
            acc_send[g * group : (g + 1) * group, r] = part.astype(BF16).reshape(group, TREE, HD)
    packed = jnp.zeros((count * TREE, HD), F32)
    for i, piece in enumerate(parts(tops) + parts(sums)):
        piece = piece.astype(F32)
        if i:
            piece = pltpu.roll(piece, i * reqs, 1)
        packed = jnp.where(lane // reqs == i, piece, packed)
    acc_send[:, reqs] = packed.astype(BF16).reshape(count, TREE, HD)

    acc_sends = []
    for k in range(count - 1):
        copy = remote(
            acc_send.at[peers[k]], acc_recv.at[k], acc_ssem.at[k], acc_rsem.at[k], peers[k]
        )
        copy.start()
        acc_sends.append(copy)

    small_lane = iota((TREE, HD), 1)

    def as_lanes(column, fill):
        wide = jnp.full((TREE, HD), fill, F32)
        for r in range(reqs):
            wide = jnp.where(small_lane == r, column[r * TREE : (r + 1) * TREE, :], wide)
        return wide

    def as_rows(wide):
        return jnp.concatenate([wide[:, r : r + 1] for r in range(reqs)], axis=0)

    def unpack(block):
        block = block.astype(F32)
        moved = [block] + [pltpu.roll(block, HD - i * reqs, 1) for i in range(1, 6)]
        return moved[0] + moved[1] + moved[2], moved[3] + moved[4] + moved[5]

    tops = [as_lanes(tree_max, 0.0)]
    sums = [as_lanes(tree_sum, 1.0)]
    for k in range(count):
        if k:
            acc_sends[k - 1].wait_recv()
        top, total = unpack(acc_recv[k - 1, reqs] if k else acc_send[me, reqs])
        tops.append(jnp.where(small_lane < reqs, top, FLOOR))
        sums.append(jnp.where(small_lane < reqs, total, 0.0))
    peak = functools.reduce(jnp.maximum, tops)
    factors = [jnp.exp(top - peak) for top in tops]
    denominator = functools.reduce(
        lambda a, b: a + b, [total * factor for total, factor in zip(sums, factors)]
    )
    inverse = 1.0 / denominator
    attention = tree_acc * as_rows(factors[0] * inverse)
    for k in range(count):
        part = acc_recv[k - 1, pl.ds(0, reqs)] if k else acc_send[me, pl.ds(0, reqs)]
        attention = attention + part.reshape(rows, HD).astype(F32) * as_rows(
            factors[k + 1] * inverse
        )
    att_buf[me] = attention.astype(BF16)

    att_peers = [partner]
    for k in range(1, pairs):
        first = 2 * lax.rem(pair + k, pairs)
        att_peers += [first + parity, first + 1 - parity]
    att_sends = [
        remote(att_buf.at[me], att_buf.at[me], att_ssem.at[i], att_rsem.at[i], peer)
        for i, peer in enumerate(att_peers)
    ]
    for copy in att_sends:
        copy.start()
    for copy in wx:
        copy.wait_recv()
    for copy in wo_copies:
        copy.wait()
    att_sends[0].wait_recv()
    attention = jnp.concatenate([att_buf[2 * pair], att_buf[2 * pair + 1]], axis=1)

    hid_sends = []
    for k in range(1, pairs):
        b = lax.rem(pair + pairs - k, pairs)
        hid_send[k - 1] = matmul(attention, wo_buf[b].reshape(2 * HD, some)).astype(BF16)
        copy = remote(
            hid_send.at[k - 1],
            hid_recv.at[k - 1],
            hid_ssem.at[k - 1],
            hid_rsem.at[k - 1],
            2 * b + parity,
        )
        copy.start()
        hid_sends.append(copy)
    hidden = matmul(attention, wo_buf[pair].reshape(2 * HD, some))
    res_copy.wait()
    hidden = hidden + res_buf[:, :some].astype(F32)
    for copy in wf:
        copy.wait_recv()
    for copy in att_sends[1:]:
        copy.wait_recv()
    attention = jnp.concatenate([att_buf[h] for h in range(count)], axis=1)
    last = matmul(attention, wf_buf[...].reshape(count * HD, full)) + res_buf[:, some:].astype(F32)
    for k in range(pairs - 1):
        hid_sends[k].wait_recv()
        hidden = hidden + hid_recv[k].astype(F32)
    hidden = jnp.concatenate([hidden, last], axis=1)

    square = jnp.sum(hidden * hidden, axis=1, keepdims=True)
    diagonal = iota((rows, HD), 0) == iota((rows, HD), 1)
    sq_send[...] = jnp.broadcast_to(
        jnp.sum(jnp.where(diagonal, square, 0.0), axis=0, keepdims=True), (8, HD)
    )
    sq_sends = [
        remote(sq_send, sq_recv.at[k], sq_ssem.at[k], sq_rsem.at[k], peers[k])
        for k in range(count - 1)
    ]
    for copy in sq_sends:
        copy.start()
    out_ref[...] = hidden.astype(BF16)
    out_copy = pltpu.make_async_copy(out_ref, out_hbm, out_sem.at[0])
    out_copy.start()
    gain = gain_ref[...].astype(F32)
    gain = jnp.concatenate([gain[i : i + 1, :] for i in range(cols // HD)], axis=1)
    scaled = hidden * gain
    total = sq_send[...]
    for k in range(count - 1):
        sq_sends[k].wait_recv()
        total = total + sq_recv[k]
    mean = jnp.sum(jnp.where(diagonal, total[0:1, :], 0.0), axis=1, keepdims=True) / (cols * count)
    features = (scaled * lax.rsqrt(mean + EPS)).astype(BF16)
    draft_ref[...] = matmul(select, features).astype(BF16)

    draft_copy = pltpu.make_async_copy(draft_ref, draft_hbm, out_sem.at[1])
    draft_copy.start()
    for copies in (q_sends, wx, wf, acc_sends, att_sends, hid_sends, sq_sends):
        for copy in copies:
            copy.wait_send()
    out_copy.wait()
    draft_copy.wait()


def hand_over(out_in, draft_in, out_ref, draft_ref, sem):
    first = pltpu.make_async_copy(out_in, out_ref, sem.at[0])
    second = pltpu.make_async_copy(draft_in, draft_ref, sem.at[1])
    first.start()
    second.start()
    first.wait()
    second.wait()


def on_device(
    count,
    q_rows,
    k_cache,
    v_cache,
    k_tree,
    v_tree,
    residual,
    wo_rows,
    gain,
    parents,
    cache_len,
    accepted_node,
):
    reqs, span, width = k_cache.shape
    rows, cols = residual.shape
    pairs = count // 2
    hbm = pl.BlockSpec(memory_space=pl.ANY)
    vmem = pl.BlockSpec(memory_space=pltpu.VMEM)
    dma = pltpu.SemaphoreType.DMA
    others = count - 1
    full = full_columns(cols)
    some = cols - full
    out_shape = (
        jax.ShapeDtypeStruct((rows, cols), BF16),
        jax.ShapeDtypeStruct((reqs * MAXACC, cols), BF16),
    )
    results = pl.pallas_call(
        functools.partial(kernel, count),
        out_shape=out_shape,
        in_specs=[hbm] * 7 + [vmem] + [hbm] * 3,
        out_specs=(hbm, hbm),
        scratch_shapes=[
            pltpu.VMEM((rows, cols), BF16),
            pltpu.VMEM((reqs * MAXACC, cols), BF16),
            pltpu.VMEM(parents.shape, jnp.int32),
            pltpu.SMEM(cache_len.shape, jnp.int32),
            pltpu.SMEM(accepted_node.shape, jnp.int32),
            pltpu.VMEM((reqs, count * TREE, HD), BF16),
            pltpu.VMEM((reqs, span, width), BF16),
            pltpu.VMEM((reqs, span, width), BF16),
            pltpu.VMEM((reqs, TREE, HD), BF16),
            pltpu.VMEM((reqs, TREE, HD), BF16),
            pltpu.VMEM((rows, cols), BF16),
            pltpu.VMEM((pairs, 2, HD, some), BF16),
            pltpu.VMEM((count, HD, full), BF16),
            pltpu.VMEM((count, reqs + 1, TREE, HD), BF16),
            pltpu.VMEM((others, reqs + 1, TREE, HD), BF16),
            pltpu.VMEM((count, rows, HD), BF16),
            pltpu.VMEM((pairs - 1, rows, some), BF16),
            pltpu.VMEM((pairs - 1, rows, some), BF16),
            pltpu.VMEM((8, HD), F32),
            pltpu.VMEM((others, 8, HD), F32),
            dma((7 + 2 * reqs,)),
            dma((pairs + 1,)),
            dma((others,)),
            dma((others,)),
            dma((others,)),
            dma((others,)),
            dma((pairs,)),
            dma((pairs,)),
            dma((others,)),
            dma((others,)),
            dma((others,)),
            dma((others,)),
            dma((pairs - 1,)),
            dma((pairs - 1,)),
            dma((others,)),
            dma((others,)),
            dma((2,)),
        ],
        compiler_params=pltpu.CompilerParams(
            collective_id=0, has_side_effects=True, vmem_limit_bytes=56 * 2**20
        ),
        name="verify",
    )(
        q_rows.reshape(reqs, TREE, HD),
        k_cache,
        v_cache,
        k_tree,
        v_tree,
        residual,
        wo_rows,
        gain.reshape(cols // HD, HD),
        parents,
        cache_len,
        accepted_node,
    )
    layer_out, draft_feat = pl.pallas_call(
        hand_over,
        out_shape=out_shape,
        in_specs=[hbm] * 2,
        out_specs=(hbm, hbm),
        scratch_shapes=[dma((2,))],
        name="hand_over",
    )(*results)
    return layer_out, draft_feat.reshape(reqs, MAXACC, cols)


def solution(mesh):
    return jax.shard_map(
        functools.partial(on_device, mesh.shape["tensor"]),
        mesh=mesh,
        in_specs=(
            P("dp", "tensor"),
            P("dp", "tensor", None),
            P("dp", "tensor", None),
            P("dp", None, None),
            P("dp", None, None),
            P("dp", "tensor"),
            P("tensor", None),
            P("tensor"),
            P("dp", None),
            P("dp"),
            P("dp"),
        ),
        out_specs=(P("dp", "tensor"), P("dp", None, "tensor")),
        check_vma=False,
    )
```
